128 devices in a mesh: src: 8 (over x, z_lo), shot: 16 (over z_hi, y, core).
Axes of the slice: x: 4, y: 4, z: 4 (z_hi: 2, z_lo: 2; z = z_hi * 2 + z_lo), core: 2. Of those that a mesh axis runs over, the one named last changes fastest.
Arguments:
- traces: bfloat16 [1024, 1024, 512], P('shot', 'src'), may hold values from -6 to 6
- frequency_index_list: int32 [128], replicated, may hold values from 1 to 255, as said below
- band: int32 [8, 3], replicated, may hold values 0 or 1
Outputs:
- multiples: bfloat16 [1024, 1024, 512], P('shot', 'src')
The draws below stay inside these ranges and needn't reach their ends.
Inputs may be any that keep to these rules, and one draw needn't show every extreme that they name: `frequency_index_list`: all values differ; 1 and 255 are always among them.
All inputs are finite; a program needn't handle non-finite values.
Results may differ from the reference program's by a relative error of at most 0.0076.
Values may be sent and summed in bfloat16 or wider, within the bound.
No kernel may reach another device: no remote copies, remote signals or barrier semaphores. Data moves between devices by JAX's collectives and lax.ppermute only.
A program may use at most 128 MiB of HBM per device.

```python
import math
import jax
import jax.numpy as jnp
from jax import lax

NG = 1024
NT = 512
NF = 128
BS = 128
NB = 8


def draw_frequency_index_list(key, part):
    key = jax.random.fold_in(key, 7)
    middle = jax.random.permutation(jax.random.fold_in(key, 1), NT // 2 - 3).astype(jnp.int32) + 2
    sample_values = jnp.concatenate([jnp.array([1, NT // 2 - 1], jnp.int32), middle[:NF - 2]])
    return jax.random.permutation(jax.random.fold_in(key, 2), sample_values).astype(jnp.int32)


def place_ends(values, rng, low, high):
    dims = values.shape
    index_at = [jax.random.randint(jax.random.fold_in(rng, axis), (), 0, dims[axis]) for axis in range(len(dims))]
    values = values.at[tuple(index_at)].set(low)
    longest = dims.index(max(dims))
    index_at[longest] = (index_at[longest] + 1) % dims[longest]
    return values.at[tuple(index_at)].set(high)


def block_scale(stream_key, extent, cuts, low, top_value):
    def one(dim, parts):
        steps = jax.random.uniform(jax.random.fold_in(jax.random.fold_in(stream_key, 6), dim), (parts,), jnp.float32, low / len(cuts), top_value / len(cuts))
        return jnp.repeat(jnp.exp(steps), extent[dim] // parts).reshape((-1,) + (1,) * (len(extent) - dim - 1))

    factor_of = one(*cuts[0])
    for cut in cuts[1:]:
        factor_of = factor_of * one(*cut)
    return factor_of


def centred(key, dims, width, reach, cuts=(), kind=jnp.bfloat16):
    drawn = width * jax.random.normal(key, dims, jnp.float32)
    if cuts:
        drawn = drawn * block_scale(key, dims, cuts, -0.22, 0.18)
    return jnp.clip(drawn, -reach, reach).astype(kind)


def setup_inputs(seed: int = 0) -> dict:
    seeds = jax.random.split(jax.random.key(seed), 4)
    return {
        "traces": centred(seeds[0], (NG, NG, NT), 1.0, 6.0, ((0, 16), (1, 8))),
        "frequency_index_list": draw_frequency_index_list(jax.random.fold_in(seeds[3], 71), 0),
        "band": place_ends((jax.random.randint(seeds[2], (NB, 3), 0, 3) < 2).astype(jnp.int32), jax.random.fold_in(seeds[2], 1), 0, 1),
    }


def tables(frequency_index_list):
    steps = jnp.arange(NT, dtype=jnp.int32)
    phase = (steps[:, None] * frequency_index_list[None, :]) % NT
    angle = phase.astype(jnp.float32) * (2.0 * math.pi / NT)
    return jnp.concatenate([jnp.cos(angle), -jnp.sin(angle)], 1).astype(jnp.bfloat16)


def aperture(band, column_begin, ncols):
    blocks = band.shape[0]
    row_segment = jnp.arange(NG, dtype=jnp.int32) // BS
    col_block = (column_begin + jnp.arange(ncols, dtype=jnp.int32)) // BS
    row_flags = jnp.broadcast_to(band[:, None, :], (blocks, BS, 3)).reshape(NG, 3).astype(jnp.float32)
    offset = col_block[None, :] - row_segment[:, None]
    factor = jnp.zeros((NG, ncols), jnp.float32)
    for shift_val in (-1, 0, 1):
        factor = factor + jnp.where(offset == shift_val, row_flags[:, shift_val + 1:shift_val + 2], jnp.zeros((), jnp.float32))
    return factor


def reference(traces, frequency_index_list, band):
    table = tables(frequency_index_list)
    spectra = jnp.dot(traces.reshape(NG * NG, NT), table, preferred_element_type=jnp.float32)
    spectra = (spectra * NT ** -0.5).astype(jnp.bfloat16).reshape(NG, NG, 2, NF)
    spectra = jnp.transpose(spectra, (3, 2, 0, 1))
    factor = aperture(band, 0, NG)

    def one_freq(pair):
        masked = (pair.astype(jnp.float32) * factor).astype(jnp.bfloat16)
        real_part = jnp.dot(masked[0], masked[0], preferred_element_type=jnp.float32) - jnp.dot(masked[1], masked[1], preferred_element_type=jnp.float32)
        imaginary_component = jnp.dot(masked[0], masked[1], preferred_element_type=jnp.float32) + jnp.dot(masked[1], masked[0], preferred_element_type=jnp.float32)
        return (jnp.stack([real_part, imaginary_component]) * NG ** -0.5).astype(jnp.bfloat16)

    product = lax.map(one_freq, spectra)
    product = jnp.transpose(product, (1, 0, 2, 3)).reshape(2 * NF, NG * NG)
    result = jnp.dot(product.T, table.T, preferred_element_type=jnp.float32)
    return (result * (2.0 * NT ** -0.5)).astype(jnp.bfloat16).reshape(NG, NG, NT)
```

```python
import math

import jax
import jax.numpy as jnp
from jax import lax
from jax.experimental import pallas as pl
from jax.experimental.pallas import tpu as pltpu
from jax.sharding import PartitionSpec as P

AXES = ("src", "shot")
ROWS = 16
VMEM = 56 * 1024 * 1024


def spectral_table(frequency_index_list, steps_count):
    steps = jnp.arange(steps_count, dtype=jnp.int32)
    phase = frequency_index_list[:, None] * steps[None, :] % steps_count
    angle = phase.astype(jnp.float32) * (2.0 * math.pi / steps_count)
    return jnp.concatenate([jnp.cos(angle), -jnp.sin(angle)], 0).astype(jnp.bfloat16)


def forward_kernel(scale, table_ref, traces_ref, out_ref, total_ref):
    rows, columns, steps = traces_ref.shape
    kept = out_ref.shape[0]
    table = table_ref[...]
    for pair in range(rows // 2):
        x = traces_ref[pl.ds(2 * pair, 2)].reshape(2 * columns, steps)
        y = lax.dot_general(
            table, x, (((1,), (1,)), ((), ())), preferred_element_type=jnp.float32
        ) * scale
        for h in range(2):
            total_ref[pl.ds(2 * pair + h, 2 * kept, stride=rows), :] = y[:, h * columns : (h + 1) * columns]
    for c in range(2):
        part = total_ref[pl.ds(c * kept * rows, kept * rows), :]
        out_ref[:, c] = part.reshape(kept, rows, columns).astype(out_ref.dtype)


def forward(table, traces):
    shots, columns, steps = traces.shape
    kept = table.shape[0] // 2
    return pl.pallas_call(
        lambda *refs: forward_kernel(steps ** (-0.5), *refs),
        out_shape=jax.ShapeDtypeStruct((kept, 2, shots, columns), jnp.bfloat16),
        grid=(shots // ROWS,),
        in_specs=[
            pl.BlockSpec(table.shape, lambda g: (0, 0)),
            pl.BlockSpec((ROWS, columns, steps), lambda g: (g, 0, 0)),
        ],
        out_specs=pl.BlockSpec((kept, 2, ROWS, columns), lambda g: (0, 0, g, 0)),
        scratch_shapes=[pltpu.VMEM((2 * kept * ROWS, columns), jnp.float32)],
        compiler_params=pltpu.CompilerParams(vmem_limit_bytes=VMEM),
        name="forward",
    )(table, traces)


def product_kernel(blocks, size, scale, band_ref, in_ref, out_ref, left_ref, total_ref):
    per = size // in_ref.shape[2]

    def near(k, reach):
        return range(max(0, k - reach), min(blocks, k + reach + 1))

    for k in range(blocks):
        for b in near(k, 1):
            flag = band_ref[b, k - b + 1].astype(jnp.float32)
            for c in range(2):
                x = in_ref[pl.ds((k * blocks + b) * per, per), c].reshape(size, size)
                left_ref[k, pl.ds(b * size, size), pl.ds(c * size, size)] = (
                    x.astype(jnp.float32) * flag
                ).astype(jnp.bfloat16)
    for col in range(blocks):
        total_ref[...] = jnp.zeros_like(total_ref)
        for k in near(col, 1):
            rows = near(k, 1)
            x = left_ref[col, pl.ds(k * size, size), :]
            turned = jnp.concatenate([-x[:, size:], x[:, :size]], axis=1)
            right = jnp.concatenate([x, turned], axis=0)
            left = left_ref[k, pl.ds(rows[0] * size, len(rows) * size), :]
            total_ref[pl.ds(rows[0] * size, len(rows) * size), :] += jnp.dot(
                left, right, preferred_element_type=jnp.float32
            )
        for b in near(col, 2):
            for c in range(2):
                y = total_ref[pl.ds(b * size, size), pl.ds(c * size, size)] * scale
                out_ref[pl.ds((col * blocks + b) * per, per), c] = y.astype(jnp.bfloat16).reshape(
                    per, size // per, size
                )


def product(band, gathered):
    sources, two, shots, columns = gathered.shape
    blocks = band.shape[0]
    grid_points = blocks * columns
    return pl.pallas_call(
        lambda *refs: product_kernel(blocks, columns, grid_points ** (-0.5), *refs),
        out_shape=jax.ShapeDtypeStruct(gathered.shape, jnp.bfloat16),
        in_specs=[
            pl.BlockSpec(memory_space=pltpu.SMEM),
            pl.BlockSpec(memory_space=pltpu.VMEM),
        ],
        out_specs=pl.BlockSpec(memory_space=pltpu.VMEM),
        scratch_shapes=[
            pltpu.VMEM((blocks, grid_points, 2 * columns), jnp.bfloat16),
            pltpu.VMEM((grid_points, 2 * columns), jnp.float32),
        ],
        compiler_params=pltpu.CompilerParams(vmem_limit_bytes=VMEM),
        name="product",
    )(band, gathered)


def inverse_kernel(scale, table_ref, near_ref, in_ref, out_ref, wide_ref):
    kept, _, rows, columns = in_ref.shape

    @pl.when(near_ref[0] == 0)
    def _():
        out_ref[...] = jnp.zeros_like(out_ref)

    @pl.when(near_ref[0] != 0)
    def _():
        for c in range(2):
            wide_ref[pl.ds(c * kept * rows, kept * rows), :] = (
                in_ref[:, c].astype(jnp.float32).reshape(kept * rows, columns)
            )
        table = table_ref[...]
        for s in range(rows):
            x = wide_ref[pl.ds(s, 2 * kept, stride=rows), :].astype(jnp.bfloat16)
            y = lax.dot_general(
                x, table, (((0,), (0,)), ((), ())), preferred_element_type=jnp.float32
            )
            out_ref[s] = (y * scale).astype(out_ref.dtype)


def inverse(table, near, spectra):
    kept, two, shots, columns = spectra.shape
    steps = table.shape[1]
    return pl.pallas_call(
        lambda *refs: inverse_kernel(2.0 * steps ** (-0.5), *refs),
        out_shape=jax.ShapeDtypeStruct((shots, columns, steps), jnp.bfloat16),
        grid=(shots // ROWS,),
        in_specs=[
            pl.BlockSpec(table.shape, lambda g: (0, 0)),
            pl.BlockSpec(memory_space=pltpu.SMEM),
            pl.BlockSpec((kept, two, ROWS, columns), lambda g: (0, 0, g, 0)),
        ],
        out_specs=pl.BlockSpec((ROWS, columns, steps), lambda g: (g, 0, 0)),
        scratch_shapes=[pltpu.VMEM((2 * kept * ROWS, columns), jnp.float32)],
        compiler_params=pltpu.CompilerParams(vmem_limit_bytes=VMEM),
        name="inverse",
    )(table, near, spectra)


def per_device(traces, frequency_index_list, band):
    shots, columns, steps = traces.shape
    kept = frequency_index_list.shape[0]
    table = spectral_table(frequency_index_list, steps)
    spectra = forward(table, traces)
    gathered = lax.all_to_all(spectra, AXES, split_axis=0, concat_axis=0, tiled=True)
    made = product(band, gathered)
    back = lax.all_to_all(made, AXES, split_axis=0, concat_axis=0, tiled=True)
    row_block = lax.axis_index("shot") * shots // columns
    near = jnp.abs(row_block - lax.axis_index("src")) <= 2
    return inverse(table, near.astype(jnp.int32).reshape(1), back)


def solution(mesh):
    placed = (P("shot", "src", None), P(), P())
    return jax.shard_map(
        per_device, mesh=mesh, in_specs=placed, out_specs=P("shot", "src", None), check_vma=False
    )
```

```python
import math

import jax
import jax.numpy as jnp
from jax import lax
from jax.experimental import pallas as pl
from jax.experimental.pallas import tpu as pltpu
from jax.sharding import PartitionSpec as P

AXES = ("src", "shot")
GROUP = 16
VMEM = 28 * 1024 * 1024
FORWARD_VMEM = 54 * 1024 * 1024


def quarter_wave(theta):
    t = theta * theta
    c, s = 0.0, 0.0
    for m in range(7, -1, -1):
        c = (-1.0) ** m / math.factorial(2 * m) + c * t
        s = (-1.0) ** m / math.factorial(2 * m + 1) + s * t
    return c, s * theta


def fill_table(frequency_ref, table_ref):
    rows, steps = table_ref.shape
    kept, quarter = rows // 2, steps // 4
    frequency = jnp.broadcast_to(frequency_ref[...].astype(jnp.float32), (kept, kept)).T
    frequency = jnp.broadcast_to(frequency[:, :1], (kept, quarter)).astype(jnp.int32)
    step = lax.broadcasted_iota(jnp.int32, (kept, quarter), 1)
    phase = (frequency * step) & (steps - 1)
    turns = phase // quarter
    c, s = quarter_wave((phase - turns * quarter).astype(jnp.float32) * (2.0 * math.pi / steps))
    for q in range(4):
        turn = (turns + frequency * q) & 3
        odd, cos_flip, sin_flip = (turn & 1) == 1, (turn == 1) | (turn == 2), turn >= 2
        cos, sin = jnp.where(odd, s, c), jnp.where(odd, c, s)
        at = pl.ds(q * quarter, quarter)
        table_ref[pl.ds(0, kept), at] = jnp.where(cos_flip, -cos, cos).astype(table_ref.dtype)
        table_ref[pl.ds(kept, kept), at] = jnp.where(sin_flip, sin, -sin).astype(table_ref.dtype)


def forward_kernel(frequency_ref, traces_ref, out_ref, table_ref):
    rows, columns, steps = traces_ref.shape
    kept = out_ref.shape[0]

    @pl.when(pl.program_id(0) == 0)
    def _():
        fill_table(frequency_ref, table_ref)

    table = table_ref[...]
    made = []
    for pair in range(rows // 2):
        x = traces_ref[pl.ds(2 * pair, 2)].reshape(2 * columns, steps)
        y = lax.dot_general(
            table, x, (((1,), (1,)), ((), ())), preferred_element_type=jnp.float32
        ) * steps ** (-0.5)
        made += [y[:, :columns], y[:, columns:]]
    y = jnp.swapaxes(jnp.stack(made), 0, 1).astype(out_ref.dtype)
    for c in range(2):
        out_ref[:, c] = y[c * kept : (c + 1) * kept]


def forward(frequency_index_list, traces):
    shots, columns, steps = traces.shape
    kept = frequency_index_list.shape[0]
    return pl.pallas_call(
        forward_kernel,
        out_shape=(
            jax.ShapeDtypeStruct((kept, 2, shots, columns), jnp.bfloat16),
            jax.ShapeDtypeStruct((2 * kept, steps), jnp.bfloat16),
        ),
        grid=(shots // GROUP,),
        in_specs=[
            pl.BlockSpec((1, kept), lambda g: (0, 0)),
            pl.BlockSpec((GROUP, columns, steps), lambda g: (g, 0, 0)),
        ],
        out_specs=(
            pl.BlockSpec((kept, 2, GROUP, columns), lambda g: (0, 0, g, 0)),
            pl.BlockSpec((2 * kept, steps), lambda g: (0, 0)),
        ),
        compiler_params=pltpu.CompilerParams(vmem_limit_bytes=FORWARD_VMEM),
        name="forward",
    )(frequency_index_list.reshape(1, kept), traces)


def product_kernel(band_ref, in_ref, out_ref, left_ref, right_ref):
    blocks = band_ref.shape[1]
    size = in_ref.shape[3]
    per = size // in_ref.shape[2]
    scale = (blocks * size) ** (-0.5)

    def near(k, reach):
        return range(max(0, k - reach), min(blocks, k + reach + 1))

    for k in range(blocks):
        for b in near(k, 1):
            flag = band_ref[k - b + 1, b].astype(jnp.float32)
            for c in range(2):
                x = in_ref[pl.ds((k * blocks + b) * per, per), c].reshape(size, size)
                left_ref[k, pl.ds(b * size, size), pl.ds(c * size, size)] = (
                    x.astype(jnp.float32) * flag
                ).astype(jnp.bfloat16)
    for col in range(blocks):
        ks = near(col, 1)
        for at, k in enumerate(ks):
            x = left_ref[col, pl.ds(k * size, size), :]
            right_ref[col % 2, pl.ds(2 * at * size, size), :] = x
            right_ref[col % 2, pl.ds((2 * at + 1) * size, size), :] = jnp.concatenate(
                [-x[:, size:], x[:, :size]], axis=1
            )
        for b in near(col, 2):
            used = [k for k in ks if abs(k - b) <= 1]
            left = [left_ref[k, pl.ds(b * size, size), :] for k in used]
            right = right_ref[col % 2, pl.ds(2 * (used[0] - ks[0]) * size, 2 * len(used) * size), :]
            y = jnp.dot(
                jnp.concatenate(left, axis=1), right, preferred_element_type=jnp.float32
            ) * scale
            for c in range(2):
                out_ref[pl.ds((col * blocks + b) * per, per), c] = (
                    y[:, c * size : (c + 1) * size].astype(jnp.bfloat16).reshape(per, size // per, size)
                )


def product(band, gathered):
    sources, two, shots, columns = gathered.shape
    blocks = band.shape[0]
    return pl.pallas_call(
        product_kernel,
        out_shape=jax.ShapeDtypeStruct(gathered.shape, jnp.bfloat16),
        in_specs=[
            pl.BlockSpec(memory_space=pltpu.SMEM),
            pl.BlockSpec(memory_space=pltpu.VMEM),
        ],
        out_specs=pl.BlockSpec(memory_space=pltpu.VMEM),
        scratch_shapes=[
            pltpu.VMEM((blocks, blocks * columns, 2 * columns), jnp.bfloat16),
            pltpu.VMEM((2, 6 * columns, 2 * columns), jnp.bfloat16),
        ],
        compiler_params=pltpu.CompilerParams(vmem_limit_bytes=VMEM),
        name="product",
    )(band.T, gathered)


def inverse_kernel(table_ref, in_ref, out_ref):
    kept, _, rows, columns = in_ref.shape
    steps = table_ref.shape[1]
    row_block = lax.axis_index("shot") * (pl.num_programs(0) * rows) // columns
    near = jnp.abs(row_block - lax.axis_index("src")) <= 2

    @pl.when(jnp.logical_not(near))
    def _():
        out_ref[...] = jnp.zeros_like(out_ref)

    @pl.when(near)
    def _():
        table = table_ref[...]
        x = [jnp.swapaxes(in_ref[:, c].astype(jnp.float32), 0, 1) for c in range(2)]
        for s in range(rows):
            y = lax.dot_general(
                jnp.concatenate([x[0][s], x[1][s]], axis=0).astype(jnp.bfloat16),
                table,
                (((0,), (0,)), ((), ())),
                preferred_element_type=jnp.float32,
            )
            out_ref[s] = (y * (2.0 * steps ** (-0.5))).astype(out_ref.dtype)


def inverse(table, spectra):
    kept, two, shots, columns = spectra.shape
    steps = table.shape[1]
    return pl.pallas_call(
        inverse_kernel,
        out_shape=jax.ShapeDtypeStruct((shots, columns, steps), jnp.bfloat16),
        grid=(shots // GROUP,),
        in_specs=[
            pl.BlockSpec(table.shape, lambda g: (0, 0)),
            pl.BlockSpec((kept, two, GROUP, columns), lambda g: (0, 0, g, 0)),
        ],
        out_specs=pl.BlockSpec((GROUP, columns, steps), lambda g: (g, 0, 0)),
        compiler_params=pltpu.CompilerParams(vmem_limit_bytes=VMEM),
        name="inverse",
    )(table, spectra)


def per_device(traces, frequency_index_list, band):
    spectra, table = forward(frequency_index_list, traces)
    gathered = lax.all_to_all(spectra, AXES, split_axis=0, concat_axis=0, tiled=True)
    made = product(band, gathered)
    back = lax.all_to_all(made, AXES, split_axis=0, concat_axis=0, tiled=True)
    return inverse(table, back)


def solution(mesh):
    placed = (P("shot", "src", None), P(), P())
    return jax.shard_map(
        per_device, mesh=mesh, in_specs=placed, out_specs=P("shot", "src", None), check_vma=False
    )
```

```python
import math

import jax
import jax.numpy as jnp
from jax import lax
from jax.experimental import pallas as pl
from jax.experimental.pallas import tpu as pltpu
from jax.sharding import PartitionSpec as P

AXES = ("src", "shot")
GROUP = 16
PART = 8
VMEM = 28 * 1024 * 1024


def quarter_wave(theta):
    t = theta * theta
    c, s = 0.0, 0.0
    for m in range(7, -1, -1):
        c = (-1.0) ** m / math.factorial(2 * m) + c * t
        s = (-1.0) ** m / math.factorial(2 * m + 1) + s * t
    return c, s * theta


def fill_table(frequency_ref, table_ref):
    rows, steps = table_ref.shape
    kept, quarter = rows // 2, steps // 4
    frequency = jnp.broadcast_to(frequency_ref[...].astype(jnp.float32), (kept, kept)).T
    frequency = jnp.broadcast_to(frequency[:, :1], (kept, quarter)).astype(jnp.int32)
    step = lax.broadcasted_iota(jnp.int32, (kept, quarter), 1)
    phase = (frequency * step) & (steps - 1)
    turns = phase // quarter
    c, s = quarter_wave((phase - turns * quarter).astype(jnp.float32) * (2.0 * math.pi / steps))
    for q in range(4):
        turn = (turns + frequency * q) & 3
        odd, cos_flip, sin_flip = (turn & 1) == 1, (turn == 1) | (turn == 2), turn >= 2
        cos, sin = jnp.where(odd, s, c), jnp.where(odd, c, s)
        at = pl.ds(q * quarter, quarter)
        table_ref[pl.ds(0, kept), at] = jnp.where(cos_flip, -cos, cos).astype(table_ref.dtype)
        table_ref[pl.ds(kept, kept), at] = jnp.where(sin_flip, sin, -sin).astype(table_ref.dtype)


def forward_kernel(frequency_hbm, traces_ref, out_ref, table_ref, frequency_ref, held_ref, here, arrived):
    shots, columns, steps = traces_ref.shape
    kept = out_ref.shape[0]
    starts = range(0, shots, GROUP)
    copies = [
        pltpu.make_async_copy(traces_ref.at[pl.ds(s, GROUP)], held_ref.at[pl.ds(s, GROUP)], arrived.at[n])
        for n, s in enumerate(starts)
    ]
    first = pltpu.make_async_copy(frequency_hbm, frequency_ref, here)
    first.start()
    for copy in copies:
        copy.start()
    first.wait()
    fill_table(frequency_ref, table_ref)
    table = table_ref[...]
    for start, copy in zip(starts, copies):
        copy.wait()
        made = []
        for s in range(start, start + GROUP, 2):
            x = held_ref[pl.ds(s, 2)].reshape(2 * columns, steps)
            y = lax.dot_general(
                table, x, (((1,), (1,)), ((), ())), preferred_element_type=jnp.float32
            ) * steps ** (-0.5)
            made += [y[:, :columns], y[:, columns:]]
        y = jnp.swapaxes(jnp.stack(made), 0, 1).astype(out_ref.dtype)
        for c in range(2):
            out_ref[:, c, pl.ds(start, GROUP)] = y[c * kept : (c + 1) * kept]


def forward(frequency_index_list, traces):
    shots, columns, steps = traces.shape
    kept = frequency_index_list.shape[0]
    return pl.pallas_call(
        forward_kernel,
        out_shape=(
            jax.ShapeDtypeStruct((kept, 2, shots, columns), jnp.bfloat16),
            jax.ShapeDtypeStruct((2 * kept, steps), jnp.bfloat16),
        ),
        in_specs=[pl.BlockSpec(memory_space=pltpu.HBM)] * 2,
        out_specs=(
            pl.BlockSpec(memory_space=pltpu.VMEM),
            pl.BlockSpec(memory_space=pltpu.VMEM),
        ),
        scratch_shapes=[
            pltpu.VMEM((1, kept), jnp.int32),
            pltpu.VMEM(traces.shape, traces.dtype),
            pltpu.SemaphoreType.DMA(()),
            pltpu.SemaphoreType.DMA((shots // GROUP,)),
        ],
        compiler_params=pltpu.CompilerParams(vmem_limit_bytes=VMEM),
        name="forward",
    )(
        pltpu.with_memory_space_constraint(frequency_index_list.reshape(1, kept), pltpu.HBM),
        pltpu.with_memory_space_constraint(traces, pltpu.HBM),
    )


def product_kernel(band_ref, in_ref, out_ref, left_ref, right_ref):
    blocks = band_ref.shape[1]
    size = in_ref.shape[3]
    per = size // in_ref.shape[2]
    scale = (blocks * size) ** (-0.5)

    def near(k, reach):
        return range(max(0, k - reach), min(blocks, k + reach + 1))

    for k in range(blocks):
        for b in near(k, 1):
            flag = band_ref[k - b + 1, b].astype(jnp.float32)
            for c in range(2):
                x = in_ref[pl.ds((k * blocks + b) * per, per), c].reshape(size, size)
                left_ref[k, pl.ds(b * size, size), pl.ds(c * size, size)] = (
                    x.astype(jnp.float32) * flag
                ).astype(jnp.bfloat16)
    for col in range(blocks):
        ks = near(col, 1)
        for at, k in enumerate(ks):
            x = left_ref[col, pl.ds(k * size, size), :]
            right_ref[col % 2, pl.ds(2 * at * size, size), :] = x
            right_ref[col % 2, pl.ds((2 * at + 1) * size, size), :] = jnp.concatenate(
                [-x[:, size:], x[:, :size]], axis=1
            )
        for b in near(col, 2):
            used = [k for k in ks if abs(k - b) <= 1]
            left = [left_ref[k, pl.ds(b * size, size), :] for k in used]
            right = right_ref[col % 2, pl.ds(2 * (used[0] - ks[0]) * size, 2 * len(used) * size), :]
            y = jnp.dot(
                jnp.concatenate(left, axis=1), right, preferred_element_type=jnp.float32
            ) * scale
            for c in range(2):
                out_ref[pl.ds((col * blocks + b) * per, per), c] = (
                    y[:, c * size : (c + 1) * size].astype(jnp.bfloat16).reshape(per, size // per, size)
                )


def product(band, gathered):
    sources, two, shots, columns = gathered.shape
    blocks = band.shape[0]
    return pl.pallas_call(
        product_kernel,
        out_shape=jax.ShapeDtypeStruct(gathered.shape, jnp.bfloat16),
        in_specs=[
            pl.BlockSpec(memory_space=pltpu.SMEM),
            pl.BlockSpec(memory_space=pltpu.VMEM),
        ],
        out_specs=pl.BlockSpec(memory_space=pltpu.VMEM),
        scratch_shapes=[
            pltpu.VMEM((blocks, blocks * columns, 2 * columns), jnp.bfloat16),
            pltpu.VMEM((2, 6 * columns, 2 * columns), jnp.bfloat16),
        ],
        compiler_params=pltpu.CompilerParams(vmem_limit_bytes=VMEM),
        name="product",
    )(band.T, gathered)


def inverse_kernel(table_ref, in_ref, out_ref, held_ref, sent):
    kept, _, shots, columns = in_ref.shape
    steps = table_ref.shape[1]
    row_block = lax.axis_index("shot") * shots // columns
    near = jnp.abs(row_block - lax.axis_index("src")) <= 2
    copies = [
        pltpu.make_async_copy(held_ref.at[pl.ds(s, PART)], out_ref.at[pl.ds(s, PART)], sent.at[n])
        for n, s in enumerate(range(0, shots, PART))
    ]

    @pl.when(jnp.logical_not(near))
    def _():
        held_ref[...] = jnp.zeros_like(held_ref)
        for copy in copies:
            copy.start()

    @pl.when(near)
    def _():
        table = table_ref[...]
        for start in range(0, shots, GROUP):
            x = [jnp.swapaxes(in_ref[:, c, pl.ds(start, GROUP)], 0, 1) for c in range(2)]
            for s in range(0, GROUP, 4):
                lines = [jnp.concatenate([x[0][n], x[1][n]], axis=0).T for n in range(s, s + 4)]
                y = jnp.dot(
                    jnp.concatenate(lines, axis=0), table, preferred_element_type=jnp.float32
                ) * (2.0 * steps ** (-0.5))
                held_ref[pl.ds(start + s, 4)] = y.astype(out_ref.dtype).reshape(4, columns, steps)
                if (start + s + 4) % PART == 0:
                    copies[(start + s) // PART].start()

    for copy in copies:
        copy.wait()


def inverse(table, spectra):
    kept, two, shots, columns = spectra.shape
    steps = table.shape[1]
    return pl.pallas_call(
        inverse_kernel,
        out_shape=jax.ShapeDtypeStruct((shots, columns, steps), jnp.bfloat16),
        in_specs=[pl.BlockSpec(memory_space=pltpu.VMEM)] * 2,
        out_specs=pl.BlockSpec(memory_space=pltpu.HBM),
        scratch_shapes=[
            pltpu.VMEM((shots, columns, steps), jnp.bfloat16),
            pltpu.SemaphoreType.DMA((shots // PART,)),
        ],
        compiler_params=pltpu.CompilerParams(vmem_limit_bytes=VMEM),
        name="inverse",
    )(table, spectra)


def per_device(traces, frequency_index_list, band):
    spectra, table = forward(frequency_index_list, traces)
    gathered = lax.all_to_all(spectra, AXES, split_axis=0, concat_axis=0, tiled=True)
    made = product(band, gathered)
    back = lax.all_to_all(made, AXES, split_axis=0, concat_axis=0, tiled=True)
    return inverse(table, back)


def solution(mesh):
    placed = (P("shot", "src", None), P(), P())
    return jax.shard_map(
        per_device, mesh=mesh, in_specs=placed, out_specs=P("shot", "src", None), check_vma=False
    )
```

```python
import math

import jax
import jax.numpy as jnp
from jax import lax
from jax.experimental import pallas as pl
from jax.experimental.pallas import tpu as pltpu
from jax.sharding import PartitionSpec as P

AXES = ("src", "shot")
GROUP = 16
PART = 8
VMEM = 28 * 1024 * 1024


def quarter_wave(theta):
    t = theta * theta
    c, s = 0.0, 0.0
    for m in range(7, -1, -1):
        c = (-1.0) ** m / math.factorial(2 * m) + c * t
        s = (-1.0) ** m / math.factorial(2 * m + 1) + s * t
    return c, s * theta


def fill_table(frequency_ref, table_ref):
    rows, steps = table_ref.shape
    kept, quarter = rows // 2, steps // 4
    frequency = jnp.broadcast_to(frequency_ref[...].astype(jnp.float32), (kept, kept)).T
    frequency = jnp.broadcast_to(frequency[:, :1], (kept, quarter)).astype(jnp.int32)
    step = lax.broadcasted_iota(jnp.int32, (kept, quarter), 1)
    phase = (frequency * step) & (steps - 1)
    turns = phase // quarter
    c, s = quarter_wave((phase - turns * quarter).astype(jnp.float32) * (2.0 * math.pi / steps))
    for q in range(4):
        turn = (turns + frequency * q) & 3
        odd, cos_flip, sin_flip = (turn & 1) == 1, (turn == 1) | (turn == 2), turn >= 2
        cos, sin = jnp.where(odd, s, c), jnp.where(odd, c, s)
        at = pl.ds(q * quarter, quarter)
        table_ref[pl.ds(0, kept), at] = jnp.where(cos_flip, -cos, cos).astype(table_ref.dtype)
        table_ref[pl.ds(kept, kept), at] = jnp.where(sin_flip, sin, -sin).astype(table_ref.dtype)


def forward_kernel(frequency_hbm, traces_ref, out_ref, table_ref, frequency_ref, held_ref, here, arrived):
    shots, columns, steps = traces_ref.shape
    kept = out_ref.shape[0]
    starts = range(0, shots, GROUP)
    copies = [
        pltpu.make_async_copy(traces_ref.at[pl.ds(s, GROUP)], held_ref.at[pl.ds(s, GROUP)], arrived.at[n])
        for n, s in enumerate(starts)
    ]
    first = pltpu.make_async_copy(frequency_hbm, frequency_ref, here)
    first.start()
    copies[0].start()
    first.wait()
    for copy in copies[1:]:
        copy.start()
    fill_table(frequency_ref, table_ref)
    table = table_ref[...]
    for start, copy in zip(starts, copies):
        copy.wait()
        made = []
        for s in range(start, start + GROUP, 2):
            x = held_ref[pl.ds(s, 2)].reshape(2 * columns, steps)
            y = lax.dot_general(
                table, x, (((1,), (1,)), ((), ())), preferred_element_type=jnp.float32
            ) * steps ** (-0.5)
            made += [y[:, :columns], y[:, columns:]]
        y = jnp.swapaxes(jnp.stack(made), 0, 1).astype(out_ref.dtype)
        for c in range(2):
            out_ref[:, c, pl.ds(start, GROUP)] = y[c * kept : (c + 1) * kept]


def forward(frequency_index_list, traces):
    shots, columns, steps = traces.shape
    kept = frequency_index_list.shape[0]
    return pl.pallas_call(
        forward_kernel,
        out_shape=(
            jax.ShapeDtypeStruct((kept, 2, shots, columns), jnp.bfloat16),
            jax.ShapeDtypeStruct((2 * kept, steps), jnp.bfloat16),
        ),
        in_specs=[pl.BlockSpec(memory_space=pltpu.HBM)] * 2,
        out_specs=(
            pl.BlockSpec(memory_space=pltpu.VMEM),
            pl.BlockSpec(memory_space=pltpu.VMEM),
        ),
        scratch_shapes=[
            pltpu.VMEM((1, kept), jnp.int32),
            pltpu.VMEM(traces.shape, traces.dtype),
            pltpu.SemaphoreType.DMA(()),
            pltpu.SemaphoreType.DMA((shots // GROUP,)),
        ],
        compiler_params=pltpu.CompilerParams(vmem_limit_bytes=VMEM),
        name="forward",
    )(
        pltpu.with_memory_space_constraint(frequency_index_list.reshape(1, kept), pltpu.HBM),
        pltpu.with_memory_space_constraint(traces, pltpu.HBM),
    )


def product_kernel(band_ref, in_ref, out_ref, left_ref, right_ref):
    blocks = band_ref.shape[1]
    size = in_ref.shape[3]
    per = size // in_ref.shape[2]
    scale = (blocks * size) ** (-0.5)

    def near(k, reach):
        return range(max(0, k - reach), min(blocks, k + reach + 1))

    for k in range(blocks):
        for b in near(k, 1):
            flag = band_ref[k - b + 1, b].astype(jnp.float32)
            for c in range(2):
                x = in_ref[pl.ds((k * blocks + b) * per, per), c].reshape(size, size)
                left_ref[k, pl.ds(b * size, size), pl.ds(c * size, size)] = (
                    x.astype(jnp.float32) * flag
                ).astype(jnp.bfloat16)
    for col in range(blocks):
        ks = near(col, 1)
        for at, k in enumerate(ks):
            x = left_ref[col, pl.ds(k * size, size), :]
            right_ref[col % 2, pl.ds(2 * at * size, size), :] = x
            right_ref[col % 2, pl.ds((2 * at + 1) * size, size), :] = jnp.concatenate(
                [-x[:, size:], x[:, :size]], axis=1
            )
        for b in near(col, 2):
            used = [k for k in ks if abs(k - b) <= 1]
            left = [left_ref[k, pl.ds(b * size, size), :] for k in used]
            right = right_ref[col % 2, pl.ds(2 * (used[0] - ks[0]) * size, 2 * len(used) * size), :]
            y = jnp.dot(
                jnp.concatenate(left, axis=1), right, preferred_element_type=jnp.float32
            ) * scale
            for c in range(2):
                out_ref[pl.ds((col * blocks + b) * per, per), c] = (
                    y[:, c * size : (c + 1) * size].astype(jnp.bfloat16).reshape(per, size // per, size)
                )


def product(band, gathered):
    sources, two, shots, columns = gathered.shape
    blocks = band.shape[0]
    return pl.pallas_call(
        product_kernel,
        out_shape=jax.ShapeDtypeStruct(gathered.shape, jnp.bfloat16),
        in_specs=[
            pl.BlockSpec(memory_space=pltpu.SMEM),
            pl.BlockSpec(memory_space=pltpu.VMEM),
        ],
        out_specs=pl.BlockSpec(memory_space=pltpu.VMEM),
        scratch_shapes=[
            pltpu.VMEM((blocks, blocks * columns, 2 * columns), jnp.bfloat16),
            pltpu.VMEM((2, 6 * columns, 2 * columns), jnp.bfloat16),
        ],
        compiler_params=pltpu.CompilerParams(vmem_limit_bytes=VMEM),
        name="product",
    )(band.T, gathered)


def inverse_kernel(table_ref, in_ref, out_ref, held_ref, sent):
    kept, _, shots, columns = in_ref.shape
    steps = table_ref.shape[1]
    row_block = lax.axis_index("shot") * shots // columns
    near = jnp.abs(row_block - lax.axis_index("src")) <= 2
    copies = [
        pltpu.make_async_copy(held_ref.at[pl.ds(s, PART)], out_ref.at[pl.ds(s, PART)], sent.at[n])
        for n, s in enumerate(range(0, shots, PART))
    ]

    @pl.when(jnp.logical_not(near))
    def _():
        held_ref[...] = jnp.zeros_like(held_ref)
        for copy in copies:
            copy.start()

    @pl.when(near)
    def _():
        table = table_ref[...]
        for start in range(0, shots, GROUP):
            x = [jnp.swapaxes(in_ref[:, c, pl.ds(start, GROUP)], 0, 1) for c in range(2)]
            for s in range(0, GROUP, 4):
                lines = [jnp.concatenate([x[0][n], x[1][n]], axis=0).T for n in range(s, s + 4)]
                y = jnp.dot(
                    jnp.concatenate(lines, axis=0), table, preferred_element_type=jnp.float32
                ) * (2.0 * steps ** (-0.5))
                held_ref[pl.ds(start + s, 4)] = y.astype(out_ref.dtype).reshape(4, columns, steps)
                if (start + s + 4) % PART == 0:
                    copies[(start + s) // PART].start()

    for copy in copies:
        copy.wait()


def inverse(table, spectra):
    kept, two, shots, columns = spectra.shape
    steps = table.shape[1]
    return pl.pallas_call(
        inverse_kernel,
        out_shape=jax.ShapeDtypeStruct((shots, columns, steps), jnp.bfloat16),
        in_specs=[pl.BlockSpec(memory_space=pltpu.VMEM)] * 2,
        out_specs=pl.BlockSpec(memory_space=pltpu.HBM),
        scratch_shapes=[
            pltpu.VMEM((shots, columns, steps), jnp.bfloat16),
            pltpu.SemaphoreType.DMA((shots // PART,)),
        ],
        compiler_params=pltpu.CompilerParams(vmem_limit_bytes=VMEM),
        name="inverse",
    )(table, spectra)


def per_device(traces, frequency_index_list, band):
    spectra, table = forward(frequency_index_list, traces)
    gathered = lax.all_to_all(spectra, AXES, split_axis=0, concat_axis=0, tiled=True)
    made = product(band, gathered)
    back = lax.all_to_all(made, AXES, split_axis=0, concat_axis=0, tiled=True)
    return inverse(table, back)


def solution(mesh):
    placed = (P("shot", "src", None), P(), P())
    return jax.shard_map(
        per_device, mesh=mesh, in_specs=placed, out_specs=P("shot", "src", None), check_vma=False
    )
```

```python
import math

import jax
import jax.numpy as jnp
from jax import lax
from jax.experimental import pallas as pl
from jax.experimental.pallas import tpu as pltpu
from jax.sharding import PartitionSpec as P

AXES = ("src", "shot")
GROUP = 16
PART = 4
CHUNKS = (16, 16, 32)
VMEM = 28 * 1024 * 1024


def quarter_wave(theta):
    t = theta * theta
    c, s = 0.0, 0.0
    for m in range(7, -1, -1):
        c = (-1.0) ** m / math.factorial(2 * m) + c * t
        s = (-1.0) ** m / math.factorial(2 * m + 1) + s * t
    return c, s * theta


def fill_table(frequency_ref, table_ref):
    rows, steps = table_ref.shape
    kept, quarter = rows // 2, steps // 4
    frequency = jnp.broadcast_to(frequency_ref[...].astype(jnp.float32), (kept, kept)).T
    frequency = jnp.broadcast_to(frequency[:, :1], (kept, quarter)).astype(jnp.int32)
    step = lax.broadcasted_iota(jnp.int32, (kept, quarter), 1)
    phase = (frequency * step) & (steps - 1)
    turns = phase // quarter
    c, s = quarter_wave((phase - turns * quarter).astype(jnp.float32) * (2.0 * math.pi / steps))
    for q in range(4):
        turn = (turns + frequency * q) & 3
        odd, cos_flip, sin_flip = (turn & 1) == 1, (turn == 1) | (turn == 2), turn >= 2
        cos, sin = jnp.where(odd, s, c), jnp.where(odd, c, s)
        at = pl.ds(q * quarter, quarter)
        table_ref[pl.ds(0, kept), at] = jnp.where(cos_flip, -cos, cos).astype(table_ref.dtype)
        table_ref[pl.ds(kept, kept), at] = jnp.where(sin_flip, sin, -sin).astype(table_ref.dtype)


def forward_kernel(frequency_hbm, traces_ref, out_ref, table_ref, frequency_ref, held_ref, here, arrived):
    shots, columns, steps = traces_ref.shape
    kept = out_ref.shape[0]
    begins = [sum(CHUNKS[:n]) for n in range(len(CHUNKS))]
    copies = [
        pltpu.make_async_copy(traces_ref.at[pl.ds(s, size)], held_ref.at[pl.ds(s, size)], arrived.at[n])
        for n, (s, size) in enumerate(zip(begins, CHUNKS))
    ]
    first = pltpu.make_async_copy(frequency_hbm, frequency_ref, here)
    first.start()
    copies[0].start()
    first.wait()
    for copy in copies[1:]:
        copy.start()
    fill_table(frequency_ref, table_ref)
    table = table_ref[...]
    for start in range(0, shots, GROUP):
        if start in begins:
            copies[begins.index(start)].wait()
        made = []
        for s in range(start, start + GROUP, 2):
            x = held_ref[pl.ds(s, 2)].reshape(2 * columns, steps)
            y = lax.dot_general(
                table, x, (((1,), (1,)), ((), ())), preferred_element_type=jnp.float32
            ) * steps ** (-0.5)
            made += [y[:, :columns], y[:, columns:]]
        y = jnp.swapaxes(jnp.stack(made), 0, 1).astype(out_ref.dtype)
        for c in range(2):
            out_ref[:, c, pl.ds(start, GROUP)] = y[c * kept : (c + 1) * kept]


def forward(frequency_index_list, traces):
    shots, columns, steps = traces.shape
    kept = frequency_index_list.shape[0]
    return pl.pallas_call(
        forward_kernel,
        out_shape=(
            jax.ShapeDtypeStruct((kept, 2, shots, columns), jnp.bfloat16),
            jax.ShapeDtypeStruct((2 * kept, steps), jnp.bfloat16),
        ),
        in_specs=[pl.BlockSpec(memory_space=pltpu.HBM)] * 2,
        out_specs=(
            pl.BlockSpec(memory_space=pltpu.VMEM),
            pl.BlockSpec(memory_space=pltpu.VMEM),
        ),
        scratch_shapes=[
            pltpu.VMEM((1, kept), jnp.int32),
            pltpu.VMEM(traces.shape, traces.dtype),
            pltpu.SemaphoreType.DMA(()),
            pltpu.SemaphoreType.DMA((len(CHUNKS),)),
        ],
        compiler_params=pltpu.CompilerParams(vmem_limit_bytes=VMEM),
        name="forward",
    )(
        pltpu.with_memory_space_constraint(frequency_index_list.reshape(1, kept), pltpu.HBM),
        pltpu.with_memory_space_constraint(traces, pltpu.HBM),
    )


def product_kernel(band_ref, in_ref, out_ref, left_ref, right_ref):
    blocks = band_ref.shape[1]
    size = in_ref.shape[3]
    per = size // in_ref.shape[2]
    scale = (blocks * size) ** (-0.5)

    def near(k, reach):
        return range(max(0, k - reach), min(blocks, k + reach + 1))

    for k in range(blocks):
        for b in near(k, 1):
            flag = band_ref[k - b + 1, b].astype(jnp.float32)
            for c in range(2):
                x = in_ref[pl.ds((k * blocks + b) * per, per), c].reshape(size, size)
                left_ref[k, pl.ds(b * size, size), pl.ds(c * size, size)] = (
                    x.astype(jnp.float32) * flag
                ).astype(jnp.bfloat16)
    for col in range(blocks):
        ks = near(col, 1)
        for at, k in enumerate(ks):
            x = left_ref[col, pl.ds(k * size, size), :]
            right_ref[col % 2, pl.ds(2 * at * size, size), :] = x
            right_ref[col % 2, pl.ds((2 * at + 1) * size, size), :] = jnp.concatenate(
                [-x[:, size:], x[:, :size]], axis=1
            )
        for b in near(col, 2):
            used = [k for k in ks if abs(k - b) <= 1]
            left = [left_ref[k, pl.ds(b * size, size), :] for k in used]
            right = right_ref[col % 2, pl.ds(2 * (used[0] - ks[0]) * size, 2 * len(used) * size), :]
            y = jnp.dot(
                jnp.concatenate(left, axis=1), right, preferred_element_type=jnp.float32
            ) * scale
            for c in range(2):
                out_ref[pl.ds((col * blocks + b) * per, per), c] = (
                    y[:, c * size : (c + 1) * size].astype(jnp.bfloat16).reshape(per, size // per, size)
                )


def product(band, gathered):
    sources, two, shots, columns = gathered.shape
    blocks = band.shape[0]
    return pl.pallas_call(
        product_kernel,
        out_shape=jax.ShapeDtypeStruct(gathered.shape, jnp.bfloat16),
        in_specs=[
            pl.BlockSpec(memory_space=pltpu.SMEM),
            pl.BlockSpec(memory_space=pltpu.VMEM),
        ],
        out_specs=pl.BlockSpec(memory_space=pltpu.VMEM),
        scratch_shapes=[
            pltpu.VMEM((blocks, blocks * columns, 2 * columns), jnp.bfloat16),
            pltpu.VMEM((2, 6 * columns, 2 * columns), jnp.bfloat16),
        ],
        compiler_params=pltpu.CompilerParams(vmem_limit_bytes=VMEM),
        name="product",
    )(band.T, gathered)


def inverse_kernel(table_ref, in_ref, out_ref, held_ref, sent):
    kept, _, shots, columns = in_ref.shape
    steps = table_ref.shape[1]
    row_block = lax.axis_index("shot") * shots // columns
    near = jnp.abs(row_block - lax.axis_index("src")) <= 2
    copies = [
        pltpu.make_async_copy(held_ref.at[pl.ds(s, PART)], out_ref.at[pl.ds(s, PART)], sent.at[n])
        for n, s in enumerate(range(0, shots, PART))
    ]

    @pl.when(jnp.logical_not(near))
    def _():
        held_ref[...] = jnp.zeros_like(held_ref)
        for copy in copies:
            copy.start()

    @pl.when(near)
    def _():
        table = table_ref[...]
        for start in range(0, shots, GROUP):
            x = [jnp.swapaxes(in_ref[:, c, pl.ds(start, GROUP)], 0, 1) for c in range(2)]
            for s in range(0, GROUP, 4):
                lines = [jnp.concatenate([x[0][n], x[1][n]], axis=0).T for n in range(s, s + 4)]
                y = jnp.dot(
                    jnp.concatenate(lines, axis=0), table, preferred_element_type=jnp.float32
                ) * (2.0 * steps ** (-0.5))
                held_ref[pl.ds(start + s, 4)] = y.astype(out_ref.dtype).reshape(4, columns, steps)
                if (start + s + 4) % PART == 0:
                    copies[(start + s) // PART].start()

    for copy in copies:
        copy.wait()


def inverse(table, spectra):
    kept, two, shots, columns = spectra.shape
    steps = table.shape[1]
    return pl.pallas_call(
        inverse_kernel,
        out_shape=jax.ShapeDtypeStruct((shots, columns, steps), jnp.bfloat16),
        in_specs=[pl.BlockSpec(memory_space=pltpu.VMEM)] * 2,
        out_specs=pl.BlockSpec(memory_space=pltpu.HBM),
        scratch_shapes=[
            pltpu.VMEM((shots, columns, steps), jnp.bfloat16),
            pltpu.SemaphoreType.DMA((shots // PART,)),
        ],
        compiler_params=pltpu.CompilerParams(vmem_limit_bytes=VMEM),
        name="inverse",
    )(table, spectra)


def per_device(traces, frequency_index_list, band):
    spectra, table = forward(frequency_index_list, traces)
    gathered = lax.all_to_all(spectra, AXES, split_axis=0, concat_axis=0, tiled=True)
    made = product(band, gathered)
    back = lax.all_to_all(made, AXES, split_axis=0, concat_axis=0, tiled=True)
    return inverse(table, back)


def solution(mesh):
    placed = (P("shot", "src", None), P(), P())
    return jax.shard_map(
        per_device, mesh=mesh, in_specs=placed, out_specs=P("shot", "src", None), check_vma=False
    )
```

```python
import math

import jax
import jax.numpy as jnp
from jax import lax
from jax.experimental import pallas as pl
from jax.experimental.pallas import tpu as pltpu
from jax.sharding import PartitionSpec as P

AXES = ("src", "shot")
GROUP = 16
PART = 4
CHUNKS = (16, 16, 32)
VMEM = 28 * 1024 * 1024


def quarter_wave(theta):
    t = theta * theta
    c, s = 0.0, 0.0
    for m in range(7, -1, -1):
        c = (-1.0) ** m / math.factorial(2 * m) + c * t
        s = (-1.0) ** m / math.factorial(2 * m + 1) + s * t
    return c, s * theta


def fill_table(frequency_ref, table_ref):
    rows, steps = table_ref.shape
    kept, quarter = rows // 2, steps // 4
    frequency = jnp.broadcast_to(frequency_ref[...].astype(jnp.float32), (kept, kept)).T
    frequency = jnp.broadcast_to(frequency[:, :1], (kept, quarter)).astype(jnp.int32)
    step = lax.broadcasted_iota(jnp.int32, (kept, quarter), 1)
    phase = (frequency * step) & (steps - 1)
    turns = phase // quarter
    c, s = quarter_wave((phase - turns * quarter).astype(jnp.float32) * (2.0 * math.pi / steps))
    for q in range(4):
        turn = (turns + frequency * q) & 3
        odd, cos_flip, sin_flip = (turn & 1) == 1, (turn == 1) | (turn == 2), turn >= 2
        cos, sin = jnp.where(odd, s, c), jnp.where(odd, c, s)
        at = pl.ds(q * quarter, quarter)
        table_ref[pl.ds(0, kept), at] = jnp.where(cos_flip, -cos, cos).astype(table_ref.dtype)
        table_ref[pl.ds(kept, kept), at] = jnp.where(sin_flip, sin, -sin).astype(table_ref.dtype)


def forward_kernel(frequency_hbm, traces_ref, out_ref, table_ref, frequency_ref, held_ref, here, arrived):
    shots, columns, steps = traces_ref.shape
    kept = out_ref.shape[0]
    begins = [sum(CHUNKS[:n]) for n in range(len(CHUNKS))]
    copies = [
        pltpu.make_async_copy(traces_ref.at[pl.ds(s, size)], held_ref.at[pl.ds(s, size)], arrived.at[n])
        for n, (s, size) in enumerate(zip(begins, CHUNKS))
    ]
    first = pltpu.make_async_copy(frequency_hbm, frequency_ref, here)
    first.start()
    copies[0].start()
    first.wait()
    for copy in copies[1:]:
        copy.start()
    fill_table(frequency_ref, table_ref)
    table = table_ref[...]
    for start in range(0, shots, GROUP):
        if start in begins:
            copies[begins.index(start)].wait()
        made = []
        for s in range(start, start + GROUP, 2):
            x = held_ref[pl.ds(s, 2)].reshape(2 * columns, steps)
            y = lax.dot_general(
                table, x, (((1,), (1,)), ((), ())), preferred_element_type=jnp.float32
            ) * steps ** (-0.5)
            made += [y[:, :columns], y[:, columns:]]
        y = jnp.swapaxes(jnp.stack(made), 0, 1).astype(out_ref.dtype)
        for c in range(2):
            out_ref[:, c, pl.ds(start, GROUP)] = y[c * kept : (c + 1) * kept]


def forward(frequency_index_list, traces):
    shots, columns, steps = traces.shape
    kept = frequency_index_list.shape[0]
    return pl.pallas_call(
        forward_kernel,
        out_shape=(
            jax.ShapeDtypeStruct((kept, 2, shots, columns), jnp.bfloat16),
            jax.ShapeDtypeStruct((2 * kept, steps), jnp.bfloat16),
        ),
        in_specs=[pl.BlockSpec(memory_space=pltpu.HBM)] * 2,
        out_specs=(
            pl.BlockSpec(memory_space=pltpu.VMEM),
            pl.BlockSpec(memory_space=pltpu.VMEM),
        ),
        scratch_shapes=[
            pltpu.VMEM((1, kept), jnp.int32),
            pltpu.VMEM(traces.shape, traces.dtype),
            pltpu.SemaphoreType.DMA(()),
            pltpu.SemaphoreType.DMA((len(CHUNKS),)),
        ],
        compiler_params=pltpu.CompilerParams(vmem_limit_bytes=VMEM),
        name="forward",
    )(
        pltpu.with_memory_space_constraint(frequency_index_list.reshape(1, kept), pltpu.HBM),
        pltpu.with_memory_space_constraint(traces, pltpu.HBM),
    )


def product_kernel(band_ref, in_ref, out_ref, left_ref, right_ref):
    blocks = band_ref.shape[1]
    size = in_ref.shape[3]
    per = size // in_ref.shape[2]
    scale = (blocks * size) ** (-0.5)

    def near(k, reach):
        return range(max(0, k - reach), min(blocks, k + reach + 1))

    for k in range(blocks):
        for b in near(k, 1):
            flag = band_ref[k - b + 1, b].astype(jnp.float32)
            for c in range(2):
                x = in_ref[pl.ds((k * blocks + b) * per, per), c].reshape(size, size)
                left_ref[k, pl.ds(b * size, size), pl.ds(c * size, size)] = (
                    x.astype(jnp.float32) * flag
                ).astype(jnp.bfloat16)
    for col in range(blocks):
        ks = near(col, 1)
        for at, k in enumerate(ks):
            x = left_ref[col, pl.ds(k * size, size), :]
            right_ref[col % 2, pl.ds(2 * at * size, size), :] = x
            right_ref[col % 2, pl.ds((2 * at + 1) * size, size), :] = jnp.concatenate(
                [-x[:, size:], x[:, :size]], axis=1
            )
        for b in near(col, 2):
            used = [k for k in ks if abs(k - b) <= 1]
            left = [left_ref[k, pl.ds(b * size, size), :] for k in used]
            right = right_ref[col % 2, pl.ds(2 * (used[0] - ks[0]) * size, 2 * len(used) * size), :]
            y = jnp.dot(
                jnp.concatenate(left, axis=1), right, preferred_element_type=jnp.float32
            ) * scale
            for c in range(2):
                out_ref[pl.ds((col * blocks + b) * per, per), c] = (
                    y[:, c * size : (c + 1) * size].astype(jnp.bfloat16).reshape(per, size // per, size)
                )


def product(band, gathered):
    sources, two, shots, columns = gathered.shape
    blocks = band.shape[0]
    return pl.pallas_call(
        product_kernel,
        out_shape=jax.ShapeDtypeStruct(gathered.shape, jnp.bfloat16),
        in_specs=[
            pl.BlockSpec(memory_space=pltpu.SMEM),
            pl.BlockSpec(memory_space=pltpu.VMEM),
        ],
        out_specs=pl.BlockSpec(memory_space=pltpu.VMEM),
        scratch_shapes=[
            pltpu.VMEM((blocks, blocks * columns, 2 * columns), jnp.bfloat16),
            pltpu.VMEM((2, 6 * columns, 2 * columns), jnp.bfloat16),
        ],
        compiler_params=pltpu.CompilerParams(vmem_limit_bytes=VMEM),
        name="product",
    )(band.T, gathered)


def inverse_kernel(table_ref, in_ref, out_ref, held_ref, sent):
    kept, _, shots, columns = in_ref.shape
    steps = table_ref.shape[1]
    row_block = lax.axis_index("shot") * shots // columns
    near = jnp.abs(row_block - lax.axis_index("src")) <= 2
    copies = [
        pltpu.make_async_copy(held_ref.at[pl.ds(s, PART)], out_ref.at[pl.ds(s, PART)], sent.at[n])
        for n, s in enumerate(range(0, shots, PART))
    ]

    @pl.when(jnp.logical_not(near))
    def _():
        held_ref[...] = jnp.zeros_like(held_ref)
        for copy in copies:
            copy.start()

    @pl.when(near)
    def _():
        table = table_ref[...]

        def turned(start):
            return [jnp.swapaxes(in_ref[:, c, pl.ds(start, GROUP)], 0, 1) for c in range(2)]

        after = turned(0)
        for start in range(0, shots, GROUP):
            x = after
            if start + GROUP < shots:
                after = turned(start + GROUP)
            for s in range(0, GROUP, 4):
                lines = [jnp.concatenate([x[0][n], x[1][n]], axis=0).T for n in range(s, s + 4)]
                y = jnp.dot(
                    jnp.concatenate(lines, axis=0), table, preferred_element_type=jnp.float32
                ) * (2.0 * steps ** (-0.5))
                held_ref[pl.ds(start + s, 4)] = y.astype(out_ref.dtype).reshape(4, columns, steps)
                if (start + s + 4) % PART == 0:
                    copies[(start + s) // PART].start()

    for copy in copies:
        copy.wait()


def inverse(table, spectra):
    kept, two, shots, columns = spectra.shape
    steps = table.shape[1]
    return pl.pallas_call(
        inverse_kernel,
        out_shape=jax.ShapeDtypeStruct((shots, columns, steps), jnp.bfloat16),
        in_specs=[pl.BlockSpec(memory_space=pltpu.VMEM)] * 2,
        out_specs=pl.BlockSpec(memory_space=pltpu.HBM),
        scratch_shapes=[
            pltpu.VMEM((shots, columns, steps), jnp.bfloat16),
            pltpu.SemaphoreType.DMA((shots // PART,)),
        ],
        compiler_params=pltpu.CompilerParams(vmem_limit_bytes=VMEM),
        name="inverse",
    )(table, spectra)


def per_device(traces, frequency_index_list, band):
    spectra, table = forward(frequency_index_list, traces)
    gathered = lax.all_to_all(spectra, AXES, split_axis=0, concat_axis=0, tiled=True)
    made = product(band, gathered)
    back = lax.all_to_all(made, AXES, split_axis=0, concat_axis=0, tiled=True)
    return inverse(table, back)


def solution(mesh):
    placed = (P("shot", "src", None), P(), P())
    return jax.shard_map(
        per_device, mesh=mesh, in_specs=placed, out_specs=P("shot", "src", None), check_vma=False
    )
```
